32 devices in a mesh: group: 2 (over y), fin: 4 (over z), fout: 2 (over x), rep: 2 (over core).
Axes of the slice: x: 2, y: 2, z: 4, core: 2. Of those that a mesh axis runs over, the one named last changes fastest.
Arguments:
- tokens: bfloat16 [1024, 8192], P(('group', 'rep'), 'fin'), parts along dimension 0, may hold values from -6 to 6
- weight_blocks: bfloat16 [4, 2, 448, 128, 128], P('fin', 'fout'), may hold values from -0.125 to 0.125
- block_index: int32 [4, 2, 448, 2], P('fin', 'fout'), may hold values from 0 to 55, as said below
- block_count: int32 [4, 2], P('fin', 'fout'), may hold values from 112 to 448, as said below
- cotangent: bfloat16 [1024, 14336], P(('group', 'rep', 'fin'), 'fout'), parts along dimension 0, may hold values from -6 to 6
Outputs:
- activated: bfloat16 [1024, 14336], P(('group', 'rep', 'fin'), 'fout'), parts along dimension 0
- input_grad: float32 [1024, 8192], P(('group', 'rep'), ('fin', 'fout')), parts along dimension 0
- weight_grad: float32 [8, 2, 448, 128, 128], P(('group', 'fin'), 'fout', 'rep'), parts along dimension 0
The draws below stay inside these ranges and needn't reach their ends.
There are 2 independent parts, one for each index of `group`. The reference program is written for one: setup_inputs(seed, part) draws one part's arguments, and reference() takes and returns one part's arrays. A program takes and returns all parts, laid end to end along the dimension named above; an argument that names none is the same for every part. Nothing has to cross between parts.
Inputs may be any that keep to these rules, and one draw needn't show every extreme that they name: `block_index`: within a shard the 448 slots name distinct blocks of the shard's 16 x 56 grid as (row block, column block); only the first block_count slots are listed. `block_count`: some shard lists all 448 slots.
All inputs are finite; a program needn't handle non-finite values.
Results may differ from the reference program's by a relative error of at most 0.0027.
Values may be sent and summed in bfloat16 or wider, within the bound.
A program may use at most 320 MiB of HBM per device.

```python
import jax
import jax.numpy as jnp
from jax import lax

D = 8192
FF = 14336
BLK = 128
TOKENS = 512
ROWB = 16
COLB = 56
CAP = 448
N_FIN = 4
N_FOUT = 2


def block_tables(key):
    key_score, key_first, key_second, key_top = jax.random.split(key, 4)
    tiles = ROWB * COLB
    score = jax.random.randint(key_score, (N_FIN, N_FOUT, tiles), 0, 1 << 20)
    score = score * tiles + jnp.arange(tiles, dtype=jnp.int32)
    order = jnp.argsort(score, axis=-1)[..., :CAP].astype(jnp.int32)
    index = jnp.stack([order // COLB, order % COLB], axis=-1).astype(jnp.int32)
    first = jax.random.randint(key_first, (N_FIN, N_FOUT), 0, 7)
    second = jax.random.randint(key_second, (N_FIN, N_FOUT), 0, 9)
    base = CAP // 4
    count = base + first * second * (CAP - base) // 48
    chosen = jax.random.randint(key_top, (), 0, N_FIN * N_FOUT)
    flat = jnp.arange(N_FIN * N_FOUT, dtype=jnp.int32).reshape(N_FIN, N_FOUT)
    count = jnp.where(flat == chosen, CAP, count).astype(jnp.int32)
    return (index, count)


def draw_block_index(key, part):
    return block_tables(key)[0]


def draw_block_count(key, part):
    return block_tables(key)[1]


def level_of(own_key, extent, cuts, smallest, top_value):
    gain, own = 1.0, jax.random.fold_in(own_key, 6)
    for dim, shards_of in cuts:
        heights = jnp.exp(jax.random.uniform(jax.random.fold_in(own, dim), (shards_of,), jnp.float32, smallest / len(cuts), top_value / len(cuts)))
        gain = gain * jnp.repeat(heights, extent[dim] // shards_of).reshape([-1 if axis == dim else 1 for axis in range(len(extent))])
    return gain


def gaussian(stream_key, dims, scale, reach, shards=(), kind=jnp.bfloat16):
    entries = jax.random.normal(stream_key, dims, jnp.float32) * scale
    if len(shards) > 0:
        entries = level_of(stream_key, dims, shards, -0.22, 0.18) * entries
    return jnp.clip(entries, min=-reach, max=reach).astype(kind)


def setup_inputs(seed: int = 0, part: int = 0) -> dict:
    arg_keys = jax.random.split(jax.random.key(seed), 6)
    own_keys = jax.random.split(jax.random.fold_in(arg_keys[5], part), 6)
    return {
        "tokens": gaussian(own_keys[0], (TOKENS, D), 1.0, 6.0, ((0, 2), (1, 4))),
        "weight_blocks": gaussian(arg_keys[1], (N_FIN, N_FOUT, CAP, BLK, BLK), (D // 4) ** -0.5, 0.125, ((0, 4), (1, 2))),
        "block_index": draw_block_index(jax.random.fold_in(arg_keys[5], 71), part),
        "block_count": draw_block_count(jax.random.fold_in(arg_keys[5], 71), part),
        "cotangent": gaussian(own_keys[4], (TOKENS, FF), 1.0, 6.0, ((0, 8), (1, 2))),
    }


def gelu_value(v):
    return v * (0.5 + 0.5 * lax.erf(v * 0.7071067811865476))


def gelu_slope(v):
    cdf = 0.5 + 0.5 * lax.erf(v * 0.7071067811865476)
    return cdf + v * jnp.exp(-0.5 * v * v) * 0.3989422804014327


def reference(tokens, weight_blocks, block_index, block_count, cotangent):
    high = lax.Precision.HIGHEST
    live = (jnp.arange(CAP, dtype=jnp.int32)[None, None, :] < block_count[:, :, None]).astype(jnp.float32)
    rows_hot = (block_index[..., 0][..., None] == jnp.arange(ROWB, dtype=jnp.int32)).astype(jnp.float32)
    cols_hot = (block_index[..., 1][..., None] == jnp.arange(COLB, dtype=jnp.int32)).astype(jnp.float32)
    blocks = weight_blocks.astype(jnp.float32) * live[..., None, None]
    inputs = tokens.astype(jnp.float32).reshape(TOKENS, N_FIN, ROWB, BLK)

    def forward_shard(total, shard):
        chosen = jnp.einsum('trk,ogr->togk', inputs[:, shard], rows_hot[shard], precision=high)
        product = jnp.einsum('togk,ogkn->togn', chosen, blocks[shard], precision=high)
        return total + jnp.einsum('togn,ogc->tocn', product, cols_hot[shard], precision=high), None

    start_total = jnp.zeros((TOKENS, N_FOUT, COLB, BLK), jnp.float32)
    pre, _ = lax.scan(forward_shard, start_total, jnp.arange(N_FIN, dtype=jnp.int32))
    pre = pre.reshape(TOKENS, FF)
    activated = gelu_value(pre).astype(jnp.bfloat16)
    saved = lax.optimization_barrier(pre.astype(jnp.bfloat16)).astype(jnp.float32)
    grad_pre = (cotangent.astype(jnp.float32) * gelu_slope(saved)).astype(jnp.bfloat16)
    grads = lax.optimization_barrier(grad_pre).astype(jnp.float32).reshape(TOKENS, N_FOUT, COLB, BLK)

    def backward_shard(shard):
        chosen = jnp.einsum('trk,ogr->togk', inputs[:, shard], rows_hot[shard], precision=high)
        picked = jnp.einsum('tocn,ogc->togn', grads, cols_hot[shard], precision=high)
        back = jnp.einsum('togn,ogkn->togk', picked, blocks[shard], precision=high)
        input_part = jnp.einsum('togk,ogr->trk', back, rows_hot[shard], precision=high)
        slot_grad = jnp.einsum('togk,togn->ogkn', chosen, picked, precision=high)
        return input_part, slot_grad * live[shard][..., None, None]

    input_parts, weight_grad = lax.map(backward_shard, jnp.arange(N_FIN, dtype=jnp.int32))
    input_grad = jnp.transpose(input_parts, (1, 0, 2, 3)).reshape(TOKENS, D)
    return activated, input_grad, weight_grad
```

```python
import functools

import jax
import jax.numpy as jnp
from jax import lax
from jax.experimental import pallas as pl
from jax.experimental.pallas import tpu as pltpu
from jax.sharding import PartitionSpec as P

BLK = 128


def gelu_value(v):
    return v * (0.5 + 0.5 * lax.erf(v * 0.7071067811865476))


def gelu_slope(v):
    cdf = 0.5 + 0.5 * lax.erf(v * 0.7071067811865476)
    return cdf + v * jnp.exp(-0.5 * v * v) * 0.3989422804014327


def divisor(n, most):
    d = most
    while n % d:
        d -= 1
    return d


def fill_dense(step, rows, cols, count, blocks, dense):
    group = blocks.shape[0]

    @pl.when(step == 0)
    def _():
        def clear(i, carry):
            dense[pl.ds(pl.multiple_of(i * BLK, BLK), BLK), :] = jnp.zeros(
                (BLK, dense.shape[1]), dense.dtype
            )
            return carry

        lax.fori_loop(0, dense.shape[0] // BLK, clear, 0)

    for j in range(group):
        slot = step * group + j

        @pl.when(slot < count[0])
        def _():
            r = pl.multiple_of(rows[slot] * BLK, BLK)
            c = pl.multiple_of(cols[slot] * BLK, BLK)
            dense[pl.ds(r, BLK), pl.ds(c, BLK)] = blocks[j]


def forward_kernel(fills, chunk, rows, cols, count, blocks, tokens, out, dense):
    step = pl.program_id(0)

    @pl.when(step < fills)
    def _():
        fill_dense(step, rows, cols, count, blocks, dense)

    @pl.when(step >= fills)
    def _():
        c = pl.multiple_of((step - fills) * chunk, chunk)
        out[...] = jnp.dot(
            tokens[...], dense[:, pl.ds(c, chunk)], preferred_element_type=jnp.float32
        )


def backward_kernel(fills, chunk, rows, cols, count, blocks, grads, out, dense):
    step = pl.program_id(0)

    @pl.when(step < fills)
    def _():
        fill_dense(step, rows, cols, count, blocks, dense)

    @pl.when(step >= fills)
    def _():
        r = pl.multiple_of((step - fills) * chunk, chunk)
        out[...] = lax.dot_general(
            grads[...],
            dense[pl.ds(r, chunk), :],
            (((1,), (1,)), ((), ())),
            preferred_element_type=jnp.float32,
        )


def dense_product(kernel, rows, cols, count, blocks, left, width_in, width_out, chunk, out_width):
    slots = blocks.shape[0]
    group = divisor(slots, 28)
    fills = slots // group
    steps = out_width // chunk
    height = left.shape[0]
    return pl.pallas_call(
        functools.partial(kernel, fills, chunk),
        out_shape=jax.ShapeDtypeStruct((height, out_width), jnp.float32),
        grid_spec=pltpu.PrefetchScalarGridSpec(
            num_scalar_prefetch=3,
            grid=(fills + steps,),
            in_specs=[
                pl.BlockSpec((group, BLK, BLK), lambda i, *_: (jnp.minimum(i, fills - 1), 0, 0)),
                pl.BlockSpec(left.shape, lambda i, *_: (0, 0)),
            ],
            out_specs=pl.BlockSpec((height, chunk), lambda i, *_: (0, jnp.maximum(i - fills, 0))),
            scratch_shapes=[pltpu.VMEM((width_in, width_out), jnp.bfloat16)],
        ),
        compiler_params=pltpu.CompilerParams(
            dimension_semantics=("arbitrary",), vmem_limit_bytes=60 * 1024 * 1024
        ),
        cost_estimate=pl.CostEstimate(
            flops=2 * height * width_in * width_out,
            bytes_accessed=2 * blocks.size + 4 * height * out_width,
            transcendentals=0,
        ),
    )(rows, cols, count, blocks, left)


def slot_kernel(group, rows, cols, count, turned, grads, out):
    step = pl.program_id(0)
    for j in range(group):
        slot = step * group + j
        live = slot < count[0]

        @pl.when(live)
        def _():
            r = pl.multiple_of(rows[slot] * BLK, BLK)
            c = pl.multiple_of(cols[slot] * BLK, BLK)
            out[j] = jnp.dot(
                turned[pl.ds(r, BLK), :],
                grads[:, pl.ds(c, BLK)],
                preferred_element_type=jnp.float32,
            )

        @pl.when(jnp.logical_not(live))
        def _():
            out[j] = jnp.zeros((BLK, BLK), jnp.float32)


def slot_products(rows, cols, count, turned, grads):
    slots = rows.shape[0]
    group = divisor(slots, 14)
    return pl.pallas_call(
        functools.partial(slot_kernel, group),
        out_shape=jax.ShapeDtypeStruct((slots, BLK, BLK), jnp.float32),
        grid_spec=pltpu.PrefetchScalarGridSpec(
            num_scalar_prefetch=3,
            grid=(slots // group,),
            in_specs=[
                pl.BlockSpec(turned.shape, lambda i, *_: (0, 0)),
                pl.BlockSpec(grads.shape, lambda i, *_: (0, 0)),
            ],
            out_specs=pl.BlockSpec((group, BLK, BLK), lambda i, *_: (i, 0, 0)),
        ),
        compiler_params=pltpu.CompilerParams(
            dimension_semantics=("arbitrary",), vmem_limit_bytes=56 * 1024 * 1024
        ),
        cost_estimate=pl.CostEstimate(
            flops=2 * slots * BLK * BLK * grads.shape[0],
            bytes_accessed=4 * slots * BLK * BLK + 2 * grads.size,
            transcendentals=0,
        ),
    )(rows, cols, count, turned, grads)


def local(tokens, weight_blocks, block_index, block_count, cotangent):
    blocks = weight_blocks[0, 0]
    rows = block_index[0, 0, :, 0]
    cols = block_index[0, 0, :, 1]
    count = block_count[0]
    slots = blocks.shape[0]
    width_in = tokens.shape[1]
    width_out = cotangent.shape[1]
    turned = lax.all_gather(tokens, "rep", axis=0, tiled=True).T
    part = dense_product(
        forward_kernel, rows, cols, count, blocks, tokens, width_in, width_out, 512, width_out
    )
    pre = lax.psum_scatter(part, "fin", scatter_dimension=0, tiled=True)
    activated = gelu_value(pre).astype(jnp.bfloat16)
    saved = pre.astype(jnp.bfloat16)
    slope = gelu_slope(lax.optimization_barrier(saved).astype(jnp.float32))
    grad_rows = (cotangent.astype(jnp.float32) * slope).astype(jnp.bfloat16)
    grads = lax.all_gather(grad_rows, "fin", axis=0, tiled=True)
    both = lax.all_gather(grads, "rep", axis=0, tiled=True)
    input_part = dense_product(
        backward_kernel, rows, cols, count, blocks, grads, width_in, width_out, 256, width_in
    )
    input_grad = lax.psum_scatter(input_part, "fout", scatter_dimension=1, tiled=True)
    half = slots // lax.axis_size("rep")
    first = lax.axis_index("rep") * half
    weight_grad = slot_products(
        lax.dynamic_slice_in_dim(rows, first, half),
        lax.dynamic_slice_in_dim(cols, first, half),
        count - first,
        turned,
        both,
    )
    return (activated, input_grad, weight_grad.reshape(1, 1, half, BLK, BLK))


def solution(mesh):
    return jax.shard_map(
        local,
        mesh=mesh,
        in_specs=(
            P(("group", "rep"), "fin"),
            P("fin", "fout", None, None, None),
            P("fin", "fout", None, None),
            P("fin", "fout"),
            P(("group", "rep", "fin"), "fout"),
        ),
        out_specs=(
            P(("group", "rep", "fin"), "fout"),
            P(("group", "rep"), ("fin", "fout")),
            P(("group", "fin"), "fout", "rep", None, None),
        ),
        check_vma=False,
    )
```

```python
import functools

import jax
import jax.numpy as jnp
from jax import lax
from jax.experimental import pallas as pl
from jax.experimental.pallas import tpu as pltpu
from jax.sharding import PartitionSpec as P

BLK = 128


def gelu_value(v):
    return v * (0.5 + 0.5 * lax.erf(v * 0.7071067811865476))


def gelu_slope(v):
    cdf = 0.5 + 0.5 * lax.erf(v * 0.7071067811865476)
    return cdf + v * jnp.exp(-0.5 * v * v) * 0.3989422804014327


def divisor(n, most):
    d = most
    while n % d:
        d -= 1
    return d


def fill_dense(step, rows, cols, count, blocks, dense):
    group = blocks.shape[0]

    @pl.when(step == 0)
    def _():
        def clear(i, carry):
            dense[pl.ds(pl.multiple_of(i * BLK, BLK), BLK), :] = jnp.zeros(
                (BLK, dense.shape[1]), dense.dtype
            )
            return carry

        lax.fori_loop(0, dense.shape[0] // BLK, clear, 0)

    for j in range(group):
        slot = step * group + j

        @pl.when(slot < count[0])
        def _():
            r = pl.multiple_of(rows[slot] * BLK, BLK)
            c = pl.multiple_of(cols[slot] * BLK, BLK)
            dense[pl.ds(r, BLK), pl.ds(c, BLK)] = blocks[j]


def forward_kernel(fills, chunk, rows, cols, count, blocks, tokens, out, kept, peak, dense, sem):
    step = pl.program_id(0)

    @pl.when(step < fills)
    def _():
        fill_dense(step, rows, cols, count, blocks, dense)

    @pl.when(step == fills)
    def _():
        pltpu.make_async_copy(dense, kept, sem).start()
        peak[...] = jnp.zeros(peak.shape, peak.dtype)

    @pl.when(step >= fills)
    def _():
        c = pl.multiple_of((step - fills) * chunk, chunk)
        part = jnp.dot(
            tokens[...], dense[:, pl.ds(c, chunk)], preferred_element_type=jnp.float32
        )
        out[...] = part
        top = jnp.max(jnp.abs(part).reshape(-1, 8, chunk), axis=0)
        for lane in range(chunk // BLK):
            peak[...] = jnp.maximum(peak[...], top[:, lane * BLK : (lane + 1) * BLK])

    @pl.when(step == pl.num_programs(0) - 1)
    def _():
        pltpu.make_async_copy(dense, kept, sem).wait()


def forward_product(rows, cols, count, blocks, tokens, width_out):
    slots = blocks.shape[0]
    group = divisor(slots, 28)
    fills = slots // group
    chunk = 512
    height, width_in = tokens.shape
    return pl.pallas_call(
        functools.partial(forward_kernel, fills, chunk),
        out_shape=(
            jax.ShapeDtypeStruct((height, width_out), jnp.float32),
            jax.ShapeDtypeStruct((width_in, width_out), jnp.bfloat16),
            jax.ShapeDtypeStruct((8, BLK), jnp.float32),
        ),
        grid_spec=pltpu.PrefetchScalarGridSpec(
            num_scalar_prefetch=3,
            grid=(fills + width_out // chunk,),
            in_specs=[
                pl.BlockSpec((group, BLK, BLK), lambda i, *_: (jnp.minimum(i, fills - 1), 0, 0)),
                pl.BlockSpec(tokens.shape, lambda i, *_: (0, 0)),
            ],
            out_specs=(
                pl.BlockSpec((height, chunk), lambda i, *_: (0, jnp.maximum(i - fills, 0))),
                pl.BlockSpec(memory_space=pl.ANY),
                pl.BlockSpec((8, BLK), lambda i, *_: (0, 0)),
            ),
            scratch_shapes=[
                pltpu.VMEM((width_in, width_out), jnp.bfloat16),
                pltpu.SemaphoreType.DMA,
            ],
        ),
        compiler_params=pltpu.CompilerParams(
            dimension_semantics=("arbitrary",), vmem_limit_bytes=60 * 1024 * 1024
        ),
        cost_estimate=pl.CostEstimate(
            flops=2 * height * width_in * width_out,
            bytes_accessed=2 * blocks.size + 4 * height * width_out + 2 * width_in * width_out,
            transcendentals=0,
        ),
    )(rows, cols, count, blocks, tokens)


def slot_kernel(group, rows, cols, count, own_tokens, far_tokens, *refs):
    *grads, out = refs
    pieces = len(grads) // 2
    width = grads[0].shape[1] // BLK
    step = pl.program_id(0)
    for j in range(group):
        slot = step * group + j
        live = slot < count[0]
        for piece in range(pieces):
            own, far = grads[piece], grads[pieces + piece]
            near = cols[slot] - piece * width

            @pl.when(live & (near >= 0) & (near < width))
            def _():
                r = pl.multiple_of(rows[slot] * BLK, BLK)
                c = pl.multiple_of(near * BLK, BLK)
                out[j] = jnp.dot(
                    own_tokens[pl.ds(r, BLK), :],
                    own[:, pl.ds(c, BLK)],
                    preferred_element_type=jnp.float32,
                ) + jnp.dot(
                    far_tokens[pl.ds(r, BLK), :],
                    far[:, pl.ds(c, BLK)],
                    preferred_element_type=jnp.float32,
                )

        @pl.when(jnp.logical_not(live))
        def _():
            out[j] = jnp.zeros((BLK, BLK), jnp.float32)


def slot_products(rows, cols, count, *whole):
    slots = rows.shape[0]
    group = divisor(slots, 14)
    return pl.pallas_call(
        functools.partial(slot_kernel, group),
        out_shape=jax.ShapeDtypeStruct((slots, BLK, BLK), jnp.float32),
        grid_spec=pltpu.PrefetchScalarGridSpec(
            num_scalar_prefetch=3,
            grid=(slots // group,),
            in_specs=[pl.BlockSpec(a.shape, lambda i, *_: (0, 0)) for a in whole],
            out_specs=pl.BlockSpec((group, BLK, BLK), lambda i, *_: (i, 0, 0)),
        ),
        compiler_params=pltpu.CompilerParams(
            dimension_semantics=("arbitrary",), vmem_limit_bytes=56 * 1024 * 1024
        ),
        cost_estimate=pl.CostEstimate(
            flops=4 * slots * BLK * BLK * whole[0].shape[1],
            bytes_accessed=4 * slots * BLK * BLK + 2 * sum(a.size for a in whole),
            transcendentals=0,
        ),
    )(rows, cols, count, *whole)


def ahead(axis):
    size = lax.axis_size(axis)
    return [(i, (i + 1) % size) for i in range(size)]


def local(tokens, weight_blocks, block_index, block_count, cotangent):
    blocks = weight_blocks[0, 0]
    rows = block_index[0, 0, :, 0]
    cols = block_index[0, 0, :, 1]
    count = block_count[0]
    slots = blocks.shape[0]
    own, width_out = cotangent.shape
    size, me = lax.axis_size("fin"), lax.axis_index("fin")
    pieces = 2
    width = width_out // pieces

    far_tokens = lax.ppermute(tokens, "rep", ahead("rep"))
    part, dense, peak = forward_product(rows, cols, count, blocks, tokens, width_out)

    most = jnp.full((8, BLK), jnp.maximum(jnp.max(peak), 1e-30), jnp.float32)

    def term(owner, piece):
        owner = lax.rem(owner + 2 * size, size)
        return lax.dynamic_slice(part, (owner * own, piece * width), (own, width))

    bound = most
    totals = [term(me - 1, piece) for piece in range(pieces)]
    for step in range(1, size):
        scale = 60000.0 / bound[0, 0]
        came = [
            lax.ppermute((total * scale).astype(jnp.float16), "fin", ahead("fin"))
            for total in totals
        ]
        bound = lax.ppermute(bound, "fin", ahead("fin"))
        back = bound[0, 0] / 60000.0
        totals = [
            came[piece].astype(jnp.float32) * back + term(me - 1 - step, piece)
            for piece in range(pieces)
        ]
        bound = bound + most

    activated, moving, gathered = [], [], []
    for piece in range(pieces):
        pre = totals[piece]
        activated.append(gelu_value(pre).astype(jnp.bfloat16))
        saved = pre.astype(jnp.bfloat16)
        slope = gelu_slope(lax.optimization_barrier(saved).astype(jnp.float32))
        share = cotangent[:, piece * width : (piece + 1) * width].astype(jnp.float32)
        moving.append((share * slope).astype(jnp.bfloat16))
        gathered.append(jnp.zeros((own * size, width), jnp.bfloat16))
    for step in range(size):
        owner = lax.rem(me - step + size, size)
        for piece in range(pieces):
            gathered[piece] = lax.dynamic_update_slice(
                gathered[piece], moving[piece], (owner * own, 0)
            )
            if step < size - 1:
                moving[piece] = lax.ppermute(moving[piece], "fin", ahead("fin"))
    far = [lax.ppermute(g, "rep", ahead("rep")) for g in gathered]

    parts = sum(
        lax.dot_general(
            gathered[piece],
            dense[:, piece * width : (piece + 1) * width],
            (((1,), (1,)), ((), ())),
            preferred_element_type=jnp.float32,
        )
        for piece in range(pieces)
    )
    input_grad = lax.psum_scatter(parts, "fout", scatter_dimension=1, tiled=True)

    half = slots // lax.axis_size("rep")
    first = lax.axis_index("rep") * half
    weight_grad = slot_products(
        lax.dynamic_slice_in_dim(rows, first, half),
        lax.dynamic_slice_in_dim(cols, first, half),
        count - first,
        tokens.T,
        far_tokens.T,
        *gathered,
        *far,
    )
    return (
        jnp.concatenate(activated, axis=1),
        input_grad,
        weight_grad.reshape(1, 1, half, BLK, BLK),
    )


def solution(mesh):
    return jax.shard_map(
        local,
        mesh=mesh,
        in_specs=(
            P(("group", "rep"), "fin"),
            P("fin", "fout", None, None, None),
            P("fin", "fout", None, None),
            P("fin", "fout"),
            P(("group", "rep", "fin"), "fout"),
        ),
        out_specs=(
            P(("group", "rep", "fin"), "fout"),
            P(("group", "rep"), ("fin", "fout")),
            P(("group", "fin"), "fout", "rep", None, None),
        ),
        check_vma=False,
    )
```

```python
import functools

import jax
import jax.numpy as jnp
from jax import lax
from jax.experimental import pallas as pl
from jax.experimental.pallas import tpu as pltpu
from jax.sharding import PartitionSpec as P

BLK = 128


def gelu_value(v):
    return v * (0.5 + 0.5 * lax.erf(v * 0.7071067811865476))


def gelu_slope(v):
    cdf = 0.5 + 0.5 * lax.erf(v * 0.7071067811865476)
    return cdf + v * jnp.exp(-0.5 * v * v) * 0.3989422804014327


def divisor(n, most):
    d = most
    while n % d:
        d -= 1
    return d


def fill_dense(step, rows, cols, count, blocks, dense):
    group = blocks.shape[0]

    @pl.when(step == 0)
    def _():
        def clear(i, carry):
            dense[pl.ds(pl.multiple_of(i * BLK, BLK), BLK), :] = jnp.zeros(
                (BLK, dense.shape[1]), dense.dtype
            )
            return carry

        lax.fori_loop(0, dense.shape[0] // BLK, clear, 0)

    for j in range(group):
        slot = step * group + j

        @pl.when(slot < count[0])
        def _():
            r = pl.multiple_of(rows[slot] * BLK, BLK)
            c = pl.multiple_of(cols[slot] * BLK, BLK)
            dense[pl.ds(r, BLK), pl.ds(c, BLK)] = blocks[j]


def forward_kernel(fills, chunk, rows, cols, count, blocks, tokens, out, kept, peak, dense, sem):
    step = pl.program_id(0)

    @pl.when(step < fills)
    def _():
        fill_dense(step, rows, cols, count, blocks, dense)

    @pl.when(step == fills)
    def _():
        pltpu.make_async_copy(dense, kept, sem).start()
        peak[...] = jnp.zeros(peak.shape, peak.dtype)

    @pl.when(step >= fills)
    def _():
        c = pl.multiple_of((step - fills) * chunk, chunk)
        part = jnp.dot(
            tokens[...], dense[:, pl.ds(c, chunk)], preferred_element_type=jnp.float32
        )
        out[...] = part
        top = jnp.max(jnp.abs(part).reshape(-1, 8, chunk), axis=0)
        for lane in range(chunk // BLK):
            peak[...] = jnp.maximum(peak[...], top[:, lane * BLK : (lane + 1) * BLK])

    @pl.when(step == pl.num_programs(0) - 1)
    def _():
        pltpu.make_async_copy(dense, kept, sem).wait()


def forward_product(rows, cols, count, blocks, tokens, width_out):
    slots = blocks.shape[0]
    group = divisor(slots, 28)
    fills = slots // group
    chunk = 512
    height, width_in = tokens.shape
    return pl.pallas_call(
        functools.partial(forward_kernel, fills, chunk),
        out_shape=(
            jax.ShapeDtypeStruct((height, width_out), jnp.float32),
            jax.ShapeDtypeStruct((width_in, width_out), jnp.bfloat16),
            jax.ShapeDtypeStruct((8, BLK), jnp.float32),
        ),
        grid_spec=pltpu.PrefetchScalarGridSpec(
            num_scalar_prefetch=3,
            grid=(fills + width_out // chunk,),
            in_specs=[
                pl.BlockSpec((group, BLK, BLK), lambda i, *_: (jnp.minimum(i, fills - 1), 0, 0)),
                pl.BlockSpec(tokens.shape, lambda i, *_: (0, 0)),
            ],
            out_specs=(
                pl.BlockSpec((height, chunk), lambda i, *_: (0, jnp.maximum(i - fills, 0))),
                pl.BlockSpec(memory_space=pl.ANY),
                pl.BlockSpec((8, BLK), lambda i, *_: (0, 0)),
            ),
            scratch_shapes=[
                pltpu.VMEM((width_in, width_out), jnp.bfloat16),
                pltpu.SemaphoreType.DMA,
            ],
        ),
        compiler_params=pltpu.CompilerParams(
            dimension_semantics=("arbitrary",), vmem_limit_bytes=60 * 1024 * 1024
        ),
        cost_estimate=pl.CostEstimate(
            flops=2 * height * width_in * width_out,
            bytes_accessed=2 * blocks.size + 4 * height * width_out + 2 * width_in * width_out,
            transcendentals=0,
        ),
    )(rows, cols, count, blocks, tokens)


def slot_kernel(group, rows, cols, count, turned, *refs):
    *grads, out, joined = refs
    pieces = len(grads) // 2
    height, width = grads[0].shape
    step = pl.program_id(0)

    @pl.when(step == 0)
    def _():
        for k, source in enumerate(grads):
            top, left = (k // pieces) * height, (k % pieces) * width

            def move(i, carry):
                here = pl.multiple_of(i * 64, 64)
                there = pl.multiple_of(top + i * 64, 64)
                joined[pl.ds(there, 64), left : left + width] = source[pl.ds(here, 64), :]
                return carry

            lax.fori_loop(0, height // 64, move, 0)

    for j in range(group):
        slot = step * group + j
        r = pl.multiple_of(rows[slot] * BLK, BLK)
        c = pl.multiple_of(cols[slot] * BLK, BLK)
        product = jnp.dot(
            turned[pl.ds(r, BLK), :],
            joined[:, pl.ds(c, BLK)],
            preferred_element_type=jnp.float32,
        )
        out[j] = jnp.where(slot < count[0], product, 0.0)


def slot_products(rows, cols, count, width_out, *whole):
    slots = rows.shape[0]
    group = divisor(slots, 14)
    return pl.pallas_call(
        functools.partial(slot_kernel, group),
        out_shape=jax.ShapeDtypeStruct((slots, BLK, BLK), jnp.float32),
        grid_spec=pltpu.PrefetchScalarGridSpec(
            num_scalar_prefetch=3,
            grid=(slots // group,),
            in_specs=[pl.BlockSpec(a.shape, lambda i, *_: (0, 0)) for a in whole],
            out_specs=pl.BlockSpec((group, BLK, BLK), lambda i, *_: (i, 0, 0)),
            scratch_shapes=[pltpu.VMEM((whole[0].shape[1], width_out), jnp.bfloat16)],
        ),
        compiler_params=pltpu.CompilerParams(
            dimension_semantics=("arbitrary",), vmem_limit_bytes=60 * 1024 * 1024
        ),
        cost_estimate=pl.CostEstimate(
            flops=2 * slots * BLK * BLK * whole[0].shape[1],
            bytes_accessed=4 * slots * BLK * BLK + 2 * sum(a.size for a in whole),
            transcendentals=0,
        ),
    )(rows, cols, count, *whole)


def ahead(axis):
    size = lax.axis_size(axis)
    return [(i, (i + 1) % size) for i in range(size)]


def local(tokens, weight_blocks, block_index, block_count, cotangent):
    blocks = weight_blocks[0, 0]
    rows = block_index[0, 0, :, 0]
    cols = block_index[0, 0, :, 1]
    count = block_count[0]
    slots = blocks.shape[0]
    own, width_out = cotangent.shape
    size, me = lax.axis_size("fin"), lax.axis_index("fin")
    pieces = 2
    width = width_out // pieces

    far_tokens = lax.ppermute(tokens, "rep", ahead("rep"))
    part, dense, peak = forward_product(rows, cols, count, blocks, tokens, width_out)

    most = jnp.full((8, BLK), jnp.maximum(jnp.max(peak), 1e-30), jnp.float32)

    def term(owner, piece):
        owner = lax.rem(owner + 2 * size, size)
        return lax.dynamic_slice(part, (owner * own, piece * width), (own, width))

    bound = most
    totals = [term(me - 1, piece) for piece in range(pieces)]
    for step in range(1, size):
        scale = 60000.0 / bound[0, 0]
        came = [
            lax.ppermute((total * scale).astype(jnp.float16), "fin", ahead("fin"))
            for total in totals
        ]
        bound = lax.ppermute(bound, "fin", ahead("fin"))
        back = bound[0, 0] / 60000.0
        totals = [
            came[piece].astype(jnp.float32) * back + term(me - 1 - step, piece)
            for piece in range(pieces)
        ]
        bound = bound + most

    activated, moving, gathered = [], [], []
    for piece in range(pieces):
        pre = totals[piece]
        activated.append(gelu_value(pre).astype(jnp.bfloat16))
        saved = pre.astype(jnp.bfloat16)
        slope = gelu_slope(lax.optimization_barrier(saved).astype(jnp.float32))
        share = cotangent[:, piece * width : (piece + 1) * width].astype(jnp.float32)
        moving.append((share * slope).astype(jnp.bfloat16))
        gathered.append(jnp.zeros((own * size, width), jnp.bfloat16))
    for step in range(size):
        owner = lax.rem(me - step + size, size)
        for piece in range(pieces):
            gathered[piece] = lax.dynamic_update_slice(
                gathered[piece], moving[piece], (owner * own, 0)
            )
            if step < size - 1:
                moving[piece] = lax.ppermute(moving[piece], "fin", ahead("fin"))
    far = [lax.ppermute(g, "rep", ahead("rep")) for g in gathered]

    parts = sum(
        lax.dot_general(
            gathered[piece],
            dense[:, piece * width : (piece + 1) * width],
            (((1,), (1,)), ((), ())),
            preferred_element_type=jnp.float32,
        )
        for piece in range(pieces)
    )
    input_grad = lax.psum_scatter(parts, "fout", scatter_dimension=1, tiled=True)

    half = slots // lax.axis_size("rep")
    first = lax.axis_index("rep") * half
    weight_grad = slot_products(
        lax.dynamic_slice_in_dim(rows, first, half),
        lax.dynamic_slice_in_dim(cols, first, half),
        count - first,
        width_out,
        jnp.concatenate([tokens, far_tokens], axis=0).T,
        *gathered,
        *far,
    )
    return (
        jnp.concatenate(activated, axis=1),
        input_grad,
        weight_grad.reshape(1, 1, half, BLK, BLK),
    )


def solution(mesh):
    return jax.shard_map(
        local,
        mesh=mesh,
        in_specs=(
            P(("group", "rep"), "fin"),
            P("fin", "fout", None, None, None),
            P("fin", "fout", None, None),
            P("fin", "fout"),
            P(("group", "rep", "fin"), "fout"),
        ),
        out_specs=(
            P(("group", "rep", "fin"), "fout"),
            P(("group", "rep"), ("fin", "fout")),
            P(("group", "fin"), "fout", "rep", None, None),
        ),
        check_vma=False,
    )
```
